32 devices in a mesh: ctx: 32 (over z, y, x, core).
Axes of the slice: x: 2, y: 2, z: 4, core: 2. Of those that a mesh axis runs over, the one named last changes fastest.
Arguments:
- queries: bfloat16 [16384, 1024], P('ctx'), may hold values from -6 to 6
- key_rows: bfloat16 [16384, 128], P('ctx'), may hold values from -6 to 6
- value_rows: bfloat16 [16384, 128], P('ctx'), may hold values from -6 to 6
- grad_out: bfloat16 [16384, 1024], P('ctx'), may hold values from -16 to 16
- attn_out: bfloat16 [16384, 1024], P('ctx'), may hold values from -6 to 6
- log_total: float32 [8, 16384], P(None, 'ctx'), as said below
- block_pair: int32 [32], P('ctx'), may hold values from 0 to 31, as said below
Outputs:
- grad_queries: bfloat16 [16384, 1024], P('ctx')
- grad_keys: bfloat16 [16384, 128], P('ctx')
- grad_values: bfloat16 [16384, 128], P('ctx')
The draws below stay inside these ranges and needn't reach their ends.
Inputs may be any that keep to these rules, and one draw needn't show every extreme that they name: `log_total`: the log of the sum of exp(scores) over the visible keys of each head and row. `block_pair`: each block number appears once.
All inputs are finite; a program needn't handle non-finite values.
Results may differ from the reference program's by a relative error of at most 0.0073.
Values may be sent and summed in bfloat16 or wider, within the bound.
A program may use at most 64 MiB of HBM per device.

```python
import jax
import jax.numpy as jnp
from jax import lax

H = 8
DH = 128
BLK = 256
STEPS = 4
TOKENS = 16384
N_CTX = 32


def draw_queries(key, part):
    noise_key = jax.random.fold_in(key, 1)
    return jnp.clip(jax.random.normal(noise_key, (TOKENS, H * DH), jnp.float32), -4.0, 4.0).astype(jnp.bfloat16)


def draw_key_rows(key, part):
    noise_key = jax.random.fold_in(key, 2)
    return jnp.clip(jax.random.normal(noise_key, (TOKENS, DH), jnp.float32), -4.0, 4.0).astype(jnp.bfloat16)


def draw_value_rows(key, part):
    noise = jax.random.normal(jax.random.fold_in(key, 6), (TOKENS, DH), jnp.float32)
    return jnp.clip(noise, -6.0, 6.0).astype(jnp.bfloat16)


def draw_block_pair(key, part):
    return jax.random.permutation(jax.random.fold_in(key, 9), N_CTX).astype(jnp.int32)


def pair_positions(block):
    offsets = jnp.arange(BLK, dtype=jnp.int32)
    return jnp.concatenate([block * BLK + offsets, (2 * N_CTX - 1 - block) * BLK + offsets])


def forward_parts(key):
    local_rows = 2 * BLK
    score_scale = DH ** (-0.5)
    query_all = draw_queries(key, 0).astype(jnp.float32).reshape(N_CTX, local_rows, H, DH)
    key_all = draw_key_rows(key, 0).astype(jnp.float32).reshape(N_CTX, local_rows, DH)
    value_all = draw_value_rows(key, 0).astype(jnp.float32).reshape(N_CTX, local_rows, DH)
    blocks = draw_block_pair(key, 0)
    lags = jnp.arange(STEPS, dtype=jnp.int32)

    def device_forward(device):
        sources = (device - lags) % N_CTX
        key_f = key_all[sources].reshape(STEPS * local_rows, DH)
        value_f = value_all[sources].reshape(STEPS * local_rows, DH)
        query_pos = pair_positions(blocks[device])
        key_pos = jax.vmap(pair_positions)(blocks[sources]).reshape(-1)
        visible = (key_pos[None, :] <= query_pos[:, None])[None]
        scores = jnp.einsum('qhd,kd->hqk', query_all[device], key_f, precision=lax.Precision.HIGHEST) * score_scale
        scores = jnp.where(visible, scores, -1e+30)
        row_max = jnp.max(scores, axis=-1, keepdims=True)
        weights = jnp.where(visible, jnp.exp(scores - row_max), 0.0)
        row_sum = jnp.sum(weights, axis=-1, keepdims=True)
        output = jnp.einsum('hqk,kd->qhd', weights / row_sum, value_f, precision=lax.Precision.HIGHEST)
        return (output, (row_max + jnp.log(row_sum))[:, :, 0])
    outputs, totals = lax.map(device_forward, jnp.arange(N_CTX, dtype=jnp.int32))
    return (outputs.reshape(TOKENS, H * DH), totals.transpose(1, 0, 2).reshape(H, TOKENS))


def draw_attn_out(key, part):
    return forward_parts(key)[0].astype(jnp.bfloat16)


def draw_log_total(key, part):
    return forward_parts(key)[1].astype(jnp.float32)


def levels(stream_key, extent, pieces, smallest, largest):
    level = 1.0
    for axis_at, parts in pieces:
        heights = jax.random.uniform(jax.random.fold_in(jax.random.fold_in(stream_key, 6), axis_at), (parts,), jnp.float32, smallest / len(pieces), largest / len(pieces))
        level = level * jnp.repeat(jnp.exp(heights), extent[axis_at] // parts).reshape((-1,) + (1,) * (len(extent) - 1 - axis_at))
    return level


def bell_draw(key, extent, width, most, cuts=(), kind=jnp.bfloat16):
    values = width * jax.random.normal(key, extent, jnp.float32)
    if cuts:
        values = values * levels(key, extent, cuts, -0.22, 0.18)
    return jnp.clip(values, -most, most).astype(kind)


def setup_inputs(seed: int = 0) -> dict:
    key_of = jax.random.split(jax.random.key(seed), 8)
    return {
        "queries": draw_queries(jax.random.fold_in(key_of[7], 71), 0),
        "key_rows": draw_key_rows(jax.random.fold_in(key_of[7], 71), 0),
        "value_rows": draw_value_rows(jax.random.fold_in(key_of[7], 71), 0),
        "grad_out": bell_draw(key_of[3], (TOKENS, H * DH), 3.0, 16.0, ((0, 32),)),
        "attn_out": draw_attn_out(jax.random.fold_in(key_of[7], 71), 0),
        "log_total": draw_log_total(jax.random.fold_in(key_of[7], 71), 0),
        "block_pair": draw_block_pair(jax.random.fold_in(key_of[7], 71), 0),
    }


def block_positions(block, cycle_size):
    offsets = jnp.arange(BLK, dtype=jnp.int32)
    return jnp.concatenate([block * BLK + offsets, (2 * cycle_size - 1 - block) * BLK + offsets])


def reference(queries, key_rows, value_rows, grad_out, attn_out, log_total, block_pair):
    cycle_size = N_CTX
    local_rows = 2 * BLK
    score_scale = DH ** -0.5
    query_all = queries.reshape(cycle_size, local_rows, H, DH)
    grad_all = grad_out.reshape(cycle_size, local_rows, H, DH)
    output_all = attn_out.reshape(cycle_size, local_rows, H, DH)
    total_all = log_total.reshape(H, cycle_size, local_rows).transpose(1, 0, 2)
    key_all = key_rows.reshape(cycle_size, local_rows, DH)
    value_all = value_rows.reshape(cycle_size, local_rows, DH)
    lags = jnp.arange(STEPS, dtype=jnp.int32)

    def device_terms(device):
        sources = (device - lags) % cycle_size
        query_f = query_all[device].astype(jnp.float32)
        grad_f = grad_all[device].astype(jnp.float32)
        output_f = output_all[device].astype(jnp.float32)
        key_f = key_all[sources].reshape(STEPS * local_rows, DH).astype(jnp.float32)
        value_f = value_all[sources].reshape(STEPS * local_rows, DH).astype(jnp.float32)
        query_pos = block_positions(block_pair[device], cycle_size)
        key_pos = jax.vmap(block_positions, in_axes=(0, None))(block_pair[sources], cycle_size).reshape(-1)
        visible = (key_pos[None, :] <= query_pos[:, None])[None]
        scores = jnp.einsum('qhd,kd->hqk', query_f, key_f) * score_scale
        probs = jnp.where(visible, jnp.exp(scores - total_all[device][:, :, None]), 0.0)
        dprobs = jnp.einsum('qhd,kd->hqk', grad_f, value_f)
        delta = jnp.einsum('qhd,qhd->hq', grad_f, output_f)[:, :, None]
        probs_b = lax.optimization_barrier(probs.astype(jnp.bfloat16)).astype(jnp.float32)
        dscores = lax.optimization_barrier((probs * (dprobs - delta) * score_scale).astype(jnp.bfloat16)).astype(jnp.float32)
        grad_query = jnp.einsum('hqk,kd->qhd', dscores, key_f).reshape(local_rows, H * DH).astype(jnp.bfloat16)
        grad_key = jnp.einsum('hqk,qhd->kd', dscores, query_f).reshape(STEPS, local_rows, DH)
        grad_value = jnp.einsum('hqk,qhd->kd', probs_b, grad_f).reshape(STEPS, local_rows, DH)
        return grad_query, grad_key, grad_value

    query_terms, key_terms, value_terms = lax.map(device_terms, jnp.arange(cycle_size, dtype=jnp.int32))
    key_total = jnp.zeros((cycle_size, local_rows, DH), jnp.float32)
    value_total = jnp.zeros((cycle_size, local_rows, DH), jnp.float32)
    for lag_index in range(STEPS):
        key_total = key_total + jnp.roll(key_terms[:, lag_index], -lag_index, axis=0)
        value_total = value_total + jnp.roll(value_terms[:, lag_index], -lag_index, axis=0)
    return (query_terms.reshape(TOKENS, H * DH),
            key_total.reshape(TOKENS, DH).astype(jnp.bfloat16),
            value_total.reshape(TOKENS, DH).astype(jnp.bfloat16))
```

```python
import functools
import math

import jax
import jax.numpy as jnp
from jax import lax
from jax.experimental import pallas as pl
from jax.experimental.pallas import tpu as pltpu
from jax.sharding import PartitionSpec as P

MESH = pl.DeviceIdType.MESH
LOG2E = math.log2(math.e)
F32 = jnp.float32
BF16 = jnp.bfloat16
UNROLL = 2


def dot_nt(a, b):
    return lax.dot_general(a, b, (((1,), (1,)), ((), ())), preferred_element_type=F32)


def dot_nn(a, b):
    return jnp.dot(a, b, preferred_element_type=F32)


def kernel(
    count, heads, tile_ref, q_hbm, k_hbm, v_hbm, g_hbm, o_hbm, l_hbm,
    gq_hbm, gk_ref, gv_ref,
    q_s, g_s, o_s, l_s, d_s, dq_s, gq_s,
    k0, k1, k2, k3, v0, v1, v2, v3, kt_s,
    t1, t2, t3,
    ck, cv, ak, av,
    sk1, sk2, sk3, sv1, sv2, sv3, rk1, rk2, rk3, rv1, rv2, rv3,
    load_sem, fsend, frecv, rsend, rrecv, tsend, trecv, osem,
):
    rows, dh = k0.shape
    half = rows // 2
    scale = dh ** (-0.5)
    me = lax.axis_index("ctx")
    even = lax.rem(me, 2) == 0
    sibling = me + 1 - 2 * lax.rem(me, 2)

    def at(shift):
        return lax.rem(me + shift + count, count)

    loads = [
        pltpu.make_async_copy(src, dst, load_sem.at[i])
        for i, (src, dst) in enumerate(
            [(k_hbm, k0), (v_hbm, v0), (q_hbm, q_s), (g_hbm, g_s), (o_hbm, o_s), (l_hbm, l_s)]
        )
    ]
    for copy in loads:
        copy.start()

    barrier = pltpu.get_barrier_semaphore()
    for shift in (1, 2, 3, -1, -2, -3):
        pl.semaphore_signal(barrier, inc=1, device_id=(at(shift),), device_id_type=MESH)
    pl.semaphore_wait(barrier, 6)

    def remote(src, dst, ssem, rsem, target):
        return pltpu.make_async_remote_copy(
            src_ref=src, dst_ref=dst, send_sem=ssem, recv_sem=rsem,
            device_id=(target,), device_id_type=MESH,
        )

    tags = [remote(tile_ref, t, tsend.at[i], trecv.at[i], at(i + 1)) for i, t in enumerate((t1, t2, t3))]
    send1 = [remote(k_hbm, k1, fsend.at[0], frecv.at[0], at(1)),
             remote(v_hbm, v1, fsend.at[1], frecv.at[1], at(1))]
    send3 = [remote(k_hbm, k3, fsend.at[4], frecv.at[4], at(3)),
             remote(v_hbm, v3, fsend.at[5], frecv.at[5], at(3))]
    relay_even = [remote(k1, k2, fsend.at[2], frecv.at[2], sibling),
                  remote(v1, v2, fsend.at[3], frecv.at[3], sibling)]
    relay_odd = [remote(k3, k2, fsend.at[2], frecv.at[2], sibling),
                 remote(v3, v2, fsend.at[3], frecv.at[3], sibling)]
    for copy in tags + send1 + send3:
        copy.start()

    for copy in loads:
        copy.wait()

    def grads(qh, gh, lh, dh_row, kk, vv, kt, mask):
        s = dot_nt(kk, qh)
        p = jnp.exp2(s * (scale * LOG2E) - lh)
        if mask is not None:
            p = jnp.where(mask, p, 0.0)
        dp = dot_nt(vv, gh)
        ds = (p * (dp - dh_row)).astype(BF16)
        return dot_nn(kt, ds), dot_nn(ds, qh), dot_nn(p.astype(BF16), gh)

    def transposed(ref):
        kt_s[...] = ref[...].astype(F32).T.astype(BF16)

    def operands(h, off):
        cols = pl.ds(pl.multiple_of(h * dh, dh), dh)
        part = pl.ds(off, half)
        return (q_s[part, cols], g_s[part, cols],
                l_s[pl.ds(h, 1), part] * LOG2E, d_s[h, 0:1, part])

    ck[...] = jnp.zeros_like(ck)
    cv[...] = jnp.zeros_like(cv)
    transposed(k0)
    lower, upper = slice(0, half), slice(half, rows)
    diagonal = (lax.broadcasted_iota(jnp.int32, (half, half), 0)
                <= lax.broadcasted_iota(jnp.int32, (half, half), 1))

    def own_step(h, _):
        cols = pl.ds(pl.multiple_of(h * dh, dh), dh)
        prod = g_s[:, cols].astype(F32) * o_s[:, cols].astype(F32)
        high = prod.astype(BF16)
        low = (prod - high.astype(F32)).astype(BF16)
        ones = jnp.ones((8, dh), BF16)
        d_s[h] = dot_nt(ones, high) + dot_nt(ones, low)
        ops_l, ops_u = operands(h, 0), operands(h, half)
        a = grads(*ops_u, k0[lower], v0[lower], kt_s[:, lower], None)
        b = grads(*ops_u, k0[upper], v0[upper], kt_s[:, upper], diagonal)
        c = grads(*ops_l, k0[lower], v0[lower], kt_s[:, lower], diagonal)
        dq_s[h, :, upper] = a[0] + b[0]
        dq_s[h, :, lower] = c[0]
        ck[lower] += a[1] + c[1]
        ck[upper] += b[1]
        cv[lower] += a[2] + c[2]
        cv[upper] += b[2]
        return 0

    lax.fori_loop(0, heads, own_step, 0, unroll=UNROLL)

    def visit(kx, vx, tag, tag_ref, sk, sv):
        tag.wait_recv()
        keep = (tag_ref[0:1, :] < tile_ref[0:1, :]).astype(jnp.int32).astype(F32)
        drop = 1.0 - keep
        keep_wide, drop_wide = jnp.concatenate([keep] * (half // dh), 1), jnp.concatenate([drop] * (half // dh), 1)
        keep_b, drop_b = keep.astype(BF16), drop.astype(BF16)
        keep_w, drop_w = keep_wide.astype(BF16), drop_wide.astype(BF16)
        transposed(kx)
        ak[...] = jnp.zeros_like(ak)
        av[...] = jnp.zeros_like(av)
        k_pick = kx[lower] * keep_b + kx[upper] * drop_b
        v_pick = vx[lower] * keep_b + vx[upper] * drop_b
        kt_pick = kt_s[:, lower] * keep_w + kt_s[:, upper] * drop_w

        def step(h, _):
            q_l, g_l, l_l, d_l = operands(h, 0)
            q_u, g_u, l_u, d_u = operands(h, half)
            a = grads(q_u, g_u, l_u, d_u, kx[lower], vx[lower], kt_s[:, lower], None)
            b = grads(
                q_l * keep_b + q_u * drop_b, g_l * keep_b + g_u * drop_b,
                l_l * keep_wide + l_u * drop_wide, d_l * keep_wide + d_u * drop_wide,
                k_pick, v_pick, kt_pick, None,
            )
            dq_s[h, :, upper] += a[0] + b[0] * drop_wide
            dq_s[h, :, lower] += b[0] * keep_wide
            ak[lower] += a[1]
            ak[upper] += b[1]
            av[lower] += a[2]
            av[upper] += b[2]
            return 0

        lax.fori_loop(0, heads, step, 0, unroll=UNROLL)
        sk[lower] = (ak[lower] + ak[upper] * keep).astype(BF16)
        sk[upper] = (ak[upper] * drop).astype(BF16)
        sv[lower] = (av[lower] + av[upper] * keep).astype(BF16)
        sv[upper] = (av[upper] * drop).astype(BF16)

    def give(sk, sv, rk, rv, index, target):
        copies = [remote(sk, rk, rsend.at[2 * index], rrecv.at[2 * index], target),
                  remote(sv, rv, rsend.at[2 * index + 1], rrecv.at[2 * index + 1], target)]
        for copy in copies:
            copy.start()
        return copies

    for copy in send1:
        copy.wait_recv()

    @pl.when(even)
    def _():
        for copy in relay_even:
            copy.start()

    visit(k1, v1, tags[0], t1, sk1, sv1)
    back1 = give(sk1, sv1, rk1, rv1, 0, at(-1))

    for copy in send3:
        copy.wait_recv()

    @pl.when(jnp.logical_not(even))
    def _():
        for copy in relay_odd:
            copy.start()

    visit(k3, v3, tags[2], t3, sk3, sv3)
    back3 = give(sk3, sv3, rk3, rv3, 2, at(-3))

    for copy in relay_even:
        copy.wait_recv()
    visit(k2, v2, tags[1], t2, sk2, sv2)
    back2 = give(sk2, sv2, rk2, rv2, 1, at(-2))

    for h in range(heads):
        gq_s[:, h * dh:(h + 1) * dh] = (dq_s[h].T * scale).astype(BF16)
    store = pltpu.make_async_copy(gq_s, gq_hbm, osem)
    store.start()

    for copy in back1 + back3 + back2:
        copy.wait_recv()
    gk_ref[...] = ((ck[...] + rk1[...].astype(F32) + rk2[...].astype(F32) + rk3[...].astype(F32))
                   * scale).astype(BF16)
    gv_ref[...] = (cv[...] + rv1[...].astype(F32) + rv2[...].astype(F32)
                   + rv3[...].astype(F32)).astype(BF16)

    for copy in tags + send1 + send3 + relay_even + back1 + back2 + back3:
        copy.wait_send()
    store.wait()


def on_device(queries, key_rows, value_rows, grad_out, attn_out, log_total, block_pair):
    rows, dh = key_rows.shape
    width = queries.shape[1]
    heads = width // dh
    count = lax.axis_size("ctx")
    tile = jnp.broadcast_to(block_pair.reshape(1, 1), (8, 128))
    vm = functools.partial(pltpu.VMEM)
    kv = vm((rows, dh), BF16)
    acc = vm((rows, dh), F32)
    wide = vm((rows, width), BF16)
    dma = pltpu.SemaphoreType.DMA
    any_spec = pl.BlockSpec(memory_space=pl.ANY)
    vmem_spec = pl.BlockSpec(memory_space=pltpu.VMEM)
    return tuple(pl.pallas_call(
        functools.partial(kernel, count, heads),
        out_shape=(
            jax.ShapeDtypeStruct((rows, width), BF16),
            jax.ShapeDtypeStruct((rows, dh), BF16),
            jax.ShapeDtypeStruct((rows, dh), BF16),
        ),
        in_specs=[vmem_spec] + [any_spec] * 6,
        out_specs=(any_spec, vmem_spec, vmem_spec),
        scratch_shapes=[
            wide, wide, wide, vm((heads, rows), F32), vm((heads, 8, rows), F32),
            vm((heads, dh, rows), F32), wide,
            *[kv] * 8, vm((dh, rows), BF16),
            *[vm((8, 128), jnp.int32)] * 3,
            *[acc] * 4,
            *[kv] * 12,
            dma((6,)), dma((6,)), dma((6,)), dma((6,)), dma((6,)),
            dma((3,)), dma((3,)), dma,
        ],
        compiler_params=pltpu.CompilerParams(
            collective_id=0, has_side_effects=True, vmem_limit_bytes=48 * 1024 * 1024,
        ),
        cost_estimate=pl.CostEstimate(flops=6 * 10**9, bytes_accessed=6 * 2**20, transcendentals=5 * 10**6),
    )(tile, queries, key_rows, value_rows, grad_out, attn_out, log_total))


def solution(mesh):
    return jax.shard_map(
        on_device,
        mesh=mesh,
        in_specs=(
            P("ctx", None),
            P("ctx", None),
            P("ctx", None),
            P("ctx", None),
            P("ctx", None),
            P(None, "ctx"),
            P("ctx"),
        ),
        out_specs=(P("ctx", None), P("ctx", None), P("ctx", None)),
        check_vma=False,
    )
```

```python
import functools
import math

import jax
import jax.numpy as jnp
from jax import lax
from jax.experimental import pallas as pl
from jax.experimental.pallas import tpu as pltpu
from jax.sharding import PartitionSpec as P

MESH = pl.DeviceIdType.MESH
LOG2E = math.log2(math.e)
F32 = jnp.float32
BF16 = jnp.bfloat16
UNROLL = 4


def dot_nt(a, b):
    return lax.dot_general(a, b, (((1,), (1,)), ((), ())), preferred_element_type=F32)


def dot_nn(a, b):
    return jnp.dot(a, b, preferred_element_type=F32)


def kernel(
    count, heads, tile_ref, q_hbm, k_hbm, v_hbm, g_hbm, o_hbm, l_hbm,
    gq_hbm, gk_ref, gv_ref,
    q_s, g_s, o_s, l_s, d_s, dq_s, gq_s,
    k0, k1, k2, k3, v0, v1, v2, v3, kt_s,
    t1, t2, t3,
    ck, cv, ak, av,
    sk1, sk2, sk3, sv1, sv2, sv3, rk1, rk2, rk3, rv1, rv2, rv3,
    load_sem, fsend, frecv, rsend, rrecv, tsend, trecv, osem,
):
    rows, dh = k0.shape
    half = rows // 2
    scale = dh ** (-0.5)
    me = lax.axis_index("ctx")
    even = lax.rem(me, 2) == 0
    sibling = me + 1 - 2 * lax.rem(me, 2)

    def at(shift):
        return lax.rem(me + shift + count, count)

    loads = [
        pltpu.make_async_copy(src, dst, load_sem.at[i])
        for i, (src, dst) in enumerate(
            [(k_hbm, k0), (v_hbm, v0), (q_hbm, q_s), (g_hbm, g_s), (o_hbm, o_s), (l_hbm, l_s)]
        )
    ]
    for copy in loads:
        copy.start()

    barrier = pltpu.get_barrier_semaphore()
    for shift in (1, 2, 3, -1, -2, -3):
        pl.semaphore_signal(barrier, inc=1, device_id=(at(shift),), device_id_type=MESH)
    pl.semaphore_wait(barrier, 6)

    def remote(src, dst, ssem, rsem, target):
        return pltpu.make_async_remote_copy(
            src_ref=src, dst_ref=dst, send_sem=ssem, recv_sem=rsem,
            device_id=(target,), device_id_type=MESH,
        )

    tags = [remote(tile_ref, t, tsend.at[i], trecv.at[i], at(i + 1)) for i, t in enumerate((t1, t2, t3))]
    send1 = [remote(k_hbm, k1, fsend.at[0], frecv.at[0], at(1)),
             remote(v_hbm, v1, fsend.at[1], frecv.at[1], at(1))]
    send3 = [remote(k_hbm, k3, fsend.at[4], frecv.at[4], at(3)),
             remote(v_hbm, v3, fsend.at[5], frecv.at[5], at(3))]
    relay_even = [remote(k1, k2, fsend.at[2], frecv.at[2], sibling),
                  remote(v1, v2, fsend.at[3], frecv.at[3], sibling)]
    relay_odd = [remote(k3, k2, fsend.at[2], frecv.at[2], sibling),
                 remote(v3, v2, fsend.at[3], frecv.at[3], sibling)]
    for copy in tags + send1 + send3:
        copy.start()

    for copy in loads:
        copy.wait()

    def grads(qh, gh, lh, dh_row, kk, vv, kt, mask):
        s = dot_nt(kk, qh)
        p = jnp.exp2(s * (scale * LOG2E) - lh)
        if mask is not None:
            p = jnp.where(mask, p, 0.0)
        dp = dot_nt(vv, gh)
        ds = (p * (dp - dh_row)).astype(BF16)
        return dot_nn(kt, ds), dot_nn(ds, qh), dot_nn(p.astype(BF16), gh)

    def transposed(ref):
        kt_s[...] = ref[...].astype(F32).T.astype(BF16)

    def operands(h, off):
        cols = pl.ds(pl.multiple_of(h * dh, dh), dh)
        part = pl.ds(off, half)
        return (q_s[part, cols], g_s[part, cols],
                l_s[pl.ds(h, 1), part] * LOG2E, d_s[h, 0:1, part])

    ck[...] = jnp.zeros_like(ck)
    cv[...] = jnp.zeros_like(cv)
    transposed(k0)
    lower, upper = slice(0, half), slice(half, rows)
    diagonal = (lax.broadcasted_iota(jnp.int32, (half, half), 0)
                <= lax.broadcasted_iota(jnp.int32, (half, half), 1))

    def own_step(h, _):
        cols = pl.ds(pl.multiple_of(h * dh, dh), dh)
        prod = g_s[:, cols].astype(F32) * o_s[:, cols].astype(F32)
        high = prod.astype(BF16)
        low = (prod - high.astype(F32)).astype(BF16)
        ones = jnp.ones((8, dh), BF16)
        d_s[h] = dot_nt(ones, high) + dot_nt(ones, low)
        ops_l, ops_u = operands(h, 0), operands(h, half)
        a = grads(*ops_u, k0[lower], v0[lower], kt_s[:, lower], None)
        b = grads(*ops_u, k0[upper], v0[upper], kt_s[:, upper], diagonal)
        c = grads(*ops_l, k0[lower], v0[lower], kt_s[:, lower], diagonal)
        dq_s[h, :, upper] = a[0] + b[0]
        dq_s[h, :, lower] = c[0]
        ck[lower] += a[1] + c[1]
        ck[upper] += b[1]
        cv[lower] += a[2] + c[2]
        cv[upper] += b[2]
        return 0

    lax.fori_loop(0, heads, own_step, 0, unroll=UNROLL)

    def visit(kx, vx, tag, tag_ref, sk, sv):
        tag.wait_recv()
        keep = (tag_ref[0:1, :] < tile_ref[0:1, :]).astype(jnp.int32).astype(F32)
        drop = 1.0 - keep
        keep_wide, drop_wide = jnp.concatenate([keep] * (half // dh), 1), jnp.concatenate([drop] * (half // dh), 1)
        keep_b, drop_b = keep.astype(BF16), drop.astype(BF16)
        keep_w, drop_w = keep_wide.astype(BF16), drop_wide.astype(BF16)
        transposed(kx)
        ak[...] = jnp.zeros_like(ak)
        av[...] = jnp.zeros_like(av)
        k_pick = kx[lower] * keep_b + kx[upper] * drop_b
        v_pick = vx[lower] * keep_b + vx[upper] * drop_b
        kt_pick = kt_s[:, lower] * keep_w + kt_s[:, upper] * drop_w

        def step(h, _):
            q_l, g_l, l_l, d_l = operands(h, 0)
            q_u, g_u, l_u, d_u = operands(h, half)
            a = grads(q_u, g_u, l_u, d_u, kx[lower], vx[lower], kt_s[:, lower], None)
            b = grads(
                q_l * keep_b + q_u * drop_b, g_l * keep_b + g_u * drop_b,
                l_l * keep_wide + l_u * drop_wide, d_l * keep_wide + d_u * drop_wide,
                k_pick, v_pick, kt_pick, None,
            )
            dq_s[h, :, upper] += a[0] + b[0] * drop_wide
            dq_s[h, :, lower] += b[0] * keep_wide
            ak[lower] += a[1]
            ak[upper] += b[1]
            av[lower] += a[2]
            av[upper] += b[2]
            return 0

        lax.fori_loop(0, heads, step, 0, unroll=UNROLL)
        sk[lower] = (ak[lower] + ak[upper] * keep).astype(BF16)
        sk[upper] = (ak[upper] * drop).astype(BF16)
        sv[lower] = (av[lower] + av[upper] * keep).astype(BF16)
        sv[upper] = (av[upper] * drop).astype(BF16)

    def give(sk, sv, rk, rv, index, target):
        copies = [remote(sk, rk, rsend.at[2 * index], rrecv.at[2 * index], target),
                  remote(sv, rv, rsend.at[2 * index + 1], rrecv.at[2 * index + 1], target)]
        for copy in copies:
            copy.start()
        return copies

    for copy in send1:
        copy.wait_recv()

    @pl.when(even)
    def _():
        for copy in relay_even:
            copy.start()

    visit(k1, v1, tags[0], t1, sk1, sv1)
    back1 = give(sk1, sv1, rk1, rv1, 0, at(-1))

    for copy in send3:
        copy.wait_recv()

    @pl.when(jnp.logical_not(even))
    def _():
        for copy in relay_odd:
            copy.start()

    visit(k3, v3, tags[2], t3, sk3, sv3)
    back3 = give(sk3, sv3, rk3, rv3, 2, at(-3))

    for copy in relay_even:
        copy.wait_recv()
    visit(k2, v2, tags[1], t2, sk2, sv2)
    back2 = give(sk2, sv2, rk2, rv2, 1, at(-2))

    for h in range(heads):
        gq_s[:, h * dh:(h + 1) * dh] = (dq_s[h].T * scale).astype(BF16)
    store = pltpu.make_async_copy(gq_s, gq_hbm, osem)
    store.start()

    for copy in back1 + back3 + back2:
        copy.wait_recv()
    gk_ref[...] = ((ck[...] + rk1[...].astype(F32) + rk2[...].astype(F32) + rk3[...].astype(F32))
                   * scale).astype(BF16)
    gv_ref[...] = (cv[...] + rv1[...].astype(F32) + rv2[...].astype(F32)
                   + rv3[...].astype(F32)).astype(BF16)

    for copy in tags + send1 + send3 + relay_even + back1 + back2 + back3:
        copy.wait_send()
    store.wait()


def on_device(queries, key_rows, value_rows, grad_out, attn_out, log_total, block_pair):
    rows, dh = key_rows.shape
    width = queries.shape[1]
    heads = width // dh
    count = lax.axis_size("ctx")
    tile = jnp.broadcast_to(block_pair.reshape(1, 1), (8, 128))
    vm = functools.partial(pltpu.VMEM)
    kv = vm((rows, dh), BF16)
    acc = vm((rows, dh), F32)
    wide = vm((rows, width), BF16)
    dma = pltpu.SemaphoreType.DMA
    any_spec = pl.BlockSpec(memory_space=pl.ANY)
    vmem_spec = pl.BlockSpec(memory_space=pltpu.VMEM)
    return tuple(pl.pallas_call(
        functools.partial(kernel, count, heads),
        out_shape=(
            jax.ShapeDtypeStruct((rows, width), BF16),
            jax.ShapeDtypeStruct((rows, dh), BF16),
            jax.ShapeDtypeStruct((rows, dh), BF16),
        ),
        in_specs=[vmem_spec] + [any_spec] * 6,
        out_specs=(any_spec, vmem_spec, vmem_spec),
        scratch_shapes=[
            wide, wide, wide, vm((heads, rows), F32), vm((heads, 8, rows), F32),
            vm((heads, dh, rows), F32), wide,
            *[kv] * 8, vm((dh, rows), BF16),
            *[vm((8, 128), jnp.int32)] * 3,
            *[acc] * 4,
            *[kv] * 12,
            dma((6,)), dma((6,)), dma((6,)), dma((6,)), dma((6,)),
            dma((3,)), dma((3,)), dma,
        ],
        compiler_params=pltpu.CompilerParams(
            collective_id=0, has_side_effects=True, vmem_limit_bytes=62 * 1024 * 1024,
        ),
        cost_estimate=pl.CostEstimate(flops=6 * 10**9, bytes_accessed=6 * 2**20, transcendentals=5 * 10**6),
    )(tile, queries, key_rows, value_rows, grad_out, attn_out, log_total))


def solution(mesh):
    return jax.shard_map(
        on_device,
        mesh=mesh,
        in_specs=(
            P("ctx", None),
            P("ctx", None),
            P("ctx", None),
            P("ctx", None),
            P("ctx", None),
            P(None, "ctx"),
            P("ctx"),
        ),
        out_specs=(P("ctx", None), P("ctx", None), P("ctx", None)),
        check_vma=False,
    )
```

```python
import functools
import math

import jax
import jax.numpy as jnp
from jax import lax
from jax.experimental import pallas as pl
from jax.experimental.pallas import tpu as pltpu
from jax.sharding import PartitionSpec as P

MESH = pl.DeviceIdType.MESH
LOG2E = math.log2(math.e)
F32 = jnp.float32
BF16 = jnp.bfloat16
UNROLL = 4


def dot_nt(a, b):
    return lax.dot_general(a, b, (((1,), (1,)), ((), ())), preferred_element_type=F32)


def dot_nn(a, b):
    return jnp.dot(a, b, preferred_element_type=F32)


def kernel(
    count, heads, tile_ref, q_hbm, k_hbm, v_hbm, g_hbm, o_hbm, l_hbm,
    gq_hbm, gk_ref, gv_ref,
    q_s, g_s, o_s, l_s, d_s, dq_s, gq_s,
    k0, k1, k2, k3, v0, v1, v2, v3, kt_s,
    t1, t2, t3,
    ck, cv, ak, av,
    sk1, sk2, sk3, sv1, sv2, sv3, rk1, rk2, rk3, rv1, rv2, rv3,
    load_sem, fsend, frecv, rsend, rrecv, tsend, trecv, osem,
):
    rows, dh = k0.shape
    half = rows // 2
    scale = dh ** (-0.5)
    me = lax.axis_index("ctx")
    even = lax.rem(me, 2) == 0
    sibling = me + 1 - 2 * lax.rem(me, 2)

    def at(shift):
        return lax.rem(me + shift + count, count)

    loads = [
        pltpu.make_async_copy(src, dst, load_sem.at[i])
        for i, (src, dst) in enumerate(
            [(k_hbm, k0), (v_hbm, v0), (q_hbm, q_s), (g_hbm, g_s), (o_hbm, o_s), (l_hbm, l_s)]
        )
    ]
    for copy in loads:
        copy.start()

    barrier = pltpu.get_barrier_semaphore()
    for shift in (1, 2, 3, -1, -2, -3):
        pl.semaphore_signal(barrier, inc=1, device_id=(at(shift),), device_id_type=MESH)
    pl.semaphore_wait(barrier, 6)

    def remote(src, dst, ssem, rsem, target):
        return pltpu.make_async_remote_copy(
            src_ref=src, dst_ref=dst, send_sem=ssem, recv_sem=rsem,
            device_id=(target,), device_id_type=MESH,
        )

    tags = [remote(tile_ref, t, tsend.at[i], trecv.at[i], at(i + 1)) for i, t in enumerate((t1, t2, t3))]
    send1 = [remote(k_hbm, k1, fsend.at[0], frecv.at[0], at(1)),
             remote(v_hbm, v1, fsend.at[1], frecv.at[1], at(1))]
    send3 = [remote(k_hbm, k3, fsend.at[4], frecv.at[4], at(3)),
             remote(v_hbm, v3, fsend.at[5], frecv.at[5], at(3))]
    relay_even = [remote(k1, k2, fsend.at[2], frecv.at[2], sibling),
                  remote(v1, v2, fsend.at[3], frecv.at[3], sibling)]
    relay_odd = [remote(k3, k2, fsend.at[2], frecv.at[2], sibling),
                 remote(v3, v2, fsend.at[3], frecv.at[3], sibling)]
    for copy in send3 + send1 + tags:
        copy.start()

    for copy in loads:
        copy.wait()

    def grads(qh, gh, lh, dh_row, kk, vv, kt, mask):
        s = dot_nt(kk, qh)
        p = jnp.exp2(s * (scale * LOG2E) - lh)
        if mask is not None:
            p = jnp.where(mask, p, 0.0)
        dp = dot_nt(vv, gh)
        ds = (p * (dp - dh_row)).astype(BF16)
        return dot_nn(kt, ds), dot_nn(ds, qh), dot_nn(p.astype(BF16), gh)

    def transposed(ref):
        kt_s[...] = ref[...].astype(F32).T.astype(BF16)

    def operands(h, off):
        cols = pl.ds(pl.multiple_of(h * dh, dh), dh)
        part = pl.ds(off, half)
        return (q_s[part, cols], g_s[part, cols],
                l_s[pl.ds(h, 1), part] * LOG2E, d_s[h, 0:1, part])

    ck[...] = jnp.zeros_like(ck)
    cv[...] = jnp.zeros_like(cv)
    transposed(k0)
    lower, upper = slice(0, half), slice(half, rows)
    diagonal = (lax.broadcasted_iota(jnp.int32, (half, half), 0)
                <= lax.broadcasted_iota(jnp.int32, (half, half), 1))

    def own_step(h, _):
        cols = pl.ds(pl.multiple_of(h * dh, dh), dh)
        prod = g_s[:, cols].astype(F32) * o_s[:, cols].astype(F32)
        high = prod.astype(BF16)
        low = (prod - high.astype(F32)).astype(BF16)
        ones = jnp.ones((8, dh), BF16)
        d_s[h] = dot_nt(ones, high) + dot_nt(ones, low)
        ops_l, ops_u = operands(h, 0), operands(h, half)
        a = grads(*ops_u, k0[lower], v0[lower], kt_s[:, lower], None)
        b = grads(*ops_u, k0[upper], v0[upper], kt_s[:, upper], diagonal)
        c = grads(*ops_l, k0[lower], v0[lower], kt_s[:, lower], diagonal)
        dq_s[h, :, upper] = a[0] + b[0]
        dq_s[h, :, lower] = c[0]
        ck[lower] += a[1] + c[1]
        ck[upper] += b[1]
        cv[lower] += a[2] + c[2]
        cv[upper] += b[2]
        return 0

    lax.fori_loop(0, heads, own_step, 0, unroll=UNROLL)

    def visit(kx, vx, tag, tag_ref, sk, sv):
        tag.wait_recv()
        keep = (tag_ref[0:1, :] < tile_ref[0:1, :]).astype(jnp.int32).astype(F32)
        drop = 1.0 - keep
        keep_wide, drop_wide = jnp.concatenate([keep] * (half // dh), 1), jnp.concatenate([drop] * (half // dh), 1)
        keep_b, drop_b = keep.astype(BF16), drop.astype(BF16)
        keep_w, drop_w = keep_wide.astype(BF16), drop_wide.astype(BF16)
        transposed(kx)
        ak[...] = jnp.zeros_like(ak)
        av[...] = jnp.zeros_like(av)
        k_pick = kx[lower] * keep_b + kx[upper] * drop_b
        v_pick = vx[lower] * keep_b + vx[upper] * drop_b
        kt_pick = kt_s[:, lower] * keep_w + kt_s[:, upper] * drop_w

        def step(h, _):
            q_l, g_l, l_l, d_l = operands(h, 0)
            q_u, g_u, l_u, d_u = operands(h, half)
            a = grads(q_u, g_u, l_u, d_u, kx[lower], vx[lower], kt_s[:, lower], None)
            b = grads(
                q_l * keep_b + q_u * drop_b, g_l * keep_b + g_u * drop_b,
                l_l * keep_wide + l_u * drop_wide, d_l * keep_wide + d_u * drop_wide,
                k_pick, v_pick, kt_pick, None,
            )
            dq_s[h, :, upper] += a[0] + b[0] * drop_wide
            dq_s[h, :, lower] += b[0] * keep_wide
            ak[lower] += a[1]
            ak[upper] += b[1]
            av[lower] += a[2]
            av[upper] += b[2]
            return 0

        lax.fori_loop(0, heads, step, 0, unroll=UNROLL)
        sk[lower] = (ak[lower] + ak[upper] * keep).astype(BF16)
        sk[upper] = (ak[upper] * drop).astype(BF16)
        sv[lower] = (av[lower] + av[upper] * keep).astype(BF16)
        sv[upper] = (av[upper] * drop).astype(BF16)

    def give(sk, sv, rk, rv, index, target):
        copies = [remote(sk, rk, rsend.at[2 * index], rrecv.at[2 * index], target),
                  remote(sv, rv, rsend.at[2 * index + 1], rrecv.at[2 * index + 1], target)]
        for copy in copies:
            copy.start()
        return copies

    for copy in send1:
        copy.wait_recv()

    @pl.when(even)
    def _():
        for copy in relay_even:
            copy.start()

    visit(k1, v1, tags[0], t1, sk1, sv1)
    back1 = give(sk1, sv1, rk1, rv1, 0, at(-1))

    for copy in send3:
        copy.wait_recv()

    @pl.when(jnp.logical_not(even))
    def _():
        for copy in relay_odd:
            copy.start()

    visit(k3, v3, tags[2], t3, sk3, sv3)
    back3 = give(sk3, sv3, rk3, rv3, 2, at(-3))

    for copy in relay_even:
        copy.wait_recv()
    visit(k2, v2, tags[1], t2, sk2, sv2)
    back2 = give(sk2, sv2, rk2, rv2, 1, at(-2))

    for h in range(heads):
        gq_s[:, h * dh:(h + 1) * dh] = (dq_s[h].T * scale).astype(BF16)
    store = pltpu.make_async_copy(gq_s, gq_hbm, osem)
    store.start()

    for copy in back1 + back3 + back2:
        copy.wait_recv()
    gk_ref[...] = ((ck[...] + rk1[...].astype(F32) + rk2[...].astype(F32) + rk3[...].astype(F32))
                   * scale).astype(BF16)
    gv_ref[...] = (cv[...] + rv1[...].astype(F32) + rv2[...].astype(F32)
                   + rv3[...].astype(F32)).astype(BF16)

    for copy in tags + send1 + send3 + relay_even + back1 + back2 + back3:
        copy.wait_send()
    store.wait()


def on_device(queries, key_rows, value_rows, grad_out, attn_out, log_total, block_pair):
    rows, dh = key_rows.shape
    width = queries.shape[1]
    heads = width // dh
    count = lax.axis_size("ctx")
    tile = jnp.broadcast_to(block_pair.reshape(1, 1), (8, 128))
    vm = functools.partial(pltpu.VMEM)
    kv = vm((rows, dh), BF16)
    acc = vm((rows, dh), F32)
    wide = vm((rows, width), BF16)
    dma = pltpu.SemaphoreType.DMA
    any_spec = pl.BlockSpec(memory_space=pl.ANY)
    vmem_spec = pl.BlockSpec(memory_space=pltpu.VMEM)
    return tuple(pl.pallas_call(
        functools.partial(kernel, count, heads),
        out_shape=(
            jax.ShapeDtypeStruct((rows, width), BF16),
            jax.ShapeDtypeStruct((rows, dh), BF16),
            jax.ShapeDtypeStruct((rows, dh), BF16),
        ),
        in_specs=[vmem_spec] + [any_spec] * 6,
        out_specs=(any_spec, vmem_spec, vmem_spec),
        scratch_shapes=[
            wide, wide, wide, vm((heads, rows), F32), vm((heads, 8, rows), F32),
            vm((heads, dh, rows), F32), wide,
            *[kv] * 8, vm((dh, rows), BF16),
            *[vm((8, 128), jnp.int32)] * 3,
            *[acc] * 4,
            *[kv] * 12,
            dma((6,)), dma((6,)), dma((6,)), dma((6,)), dma((6,)),
            dma((3,)), dma((3,)), dma,
        ],
        compiler_params=pltpu.CompilerParams(
            collective_id=0, has_side_effects=True, vmem_limit_bytes=62 * 1024 * 1024,
        ),
        cost_estimate=pl.CostEstimate(flops=6 * 10**9, bytes_accessed=6 * 2**20, transcendentals=5 * 10**6),
    )(tile, queries, key_rows, value_rows, grad_out, attn_out, log_total))


def solution(mesh):
    return jax.shard_map(
        on_device,
        mesh=mesh,
        in_specs=(
            P("ctx", None),
            P("ctx", None),
            P("ctx", None),
            P("ctx", None),
            P("ctx", None),
            P(None, "ctx"),
            P("ctx"),
        ),
        out_specs=(P("ctx", None), P("ctx", None), P("ctx", None)),
        check_vma=False,
    )
```
